32 devices in a mesh: groups: 2 (over y), blk: 16 (over z, x, core).
Axes of the slice: x: 2, y: 2, z: 4, core: 2. Of those that a mesh axis runs over, the one named last changes fastest.
Arguments:
- particles: bfloat16 [16384, 256], P(('groups', 'blk')), parts along dimension 0
- class_ids: int32 [16384], P(('groups', 'blk')), parts along dimension 0, may hold values from 0 to 63
- score_table: float32 [64, 256], replicated, may hold values from -18 to 18
- precision: float32 [256], replicated, may hold values from 0.3 to 3
- plan: int32 [4, 16], replicated, may hold values from 0 to 15, as said below
- median: float32 [2], P('groups'), parts along dimension 0, may hold values from 20.364676 to 24.89016
Outputs:
- drift: float32 [16384, 256], P(('groups', 'blk')), parts along dimension 0
The draws below stay inside these ranges and needn't reach their ends.
There are 2 independent parts, one for each index of `groups`. The reference program is written for one: setup_inputs(seed, part) draws one part's arguments, and reference() takes and returns one part's arrays. A program takes and returns all parts, laid end to end along the dimension named above; an argument that names none is the same for every part. Nothing has to cross between parts.
Inputs may be any that keep to these rules, and one draw needn't show every extreme that they name: `plan`: row r maps each block b to b xor m_r, where m_r is a power of two; the m_r of different rows differ.
All inputs are finite; a program needn't handle non-finite values.
Results may differ from the reference program's by a relative error of at most 0.0021.
Values may be sent and summed in bfloat16 or wider, within the bound.
A program may use at most 64 MiB of HBM per device.

```python
import math
import jax
import jax.numpy as jnp
from jax import lax

D = 256
CLASSES = 64
ROWS = 512
ROUNDS = 4
HOPS = 4
PARTICLES = 8192
N_BLK = 16


def crowd(key):
    class_draw = jax.random.randint(jax.random.fold_in(key, 1), (PARTICLES,), 0, CLASSES)
    centers = jax.random.normal(jax.random.fold_in(key, 2), (CLASSES, D), jnp.float32)
    return (class_draw, centers)


def shuffle_rows(subkey):
    return jax.random.permutation(subkey, ROWS)


def draw_particles(key, part):
    class_draw, centers = crowd(key)
    key = jax.random.fold_in(key, 7)
    blocks = PARTICLES // ROWS
    protos = jax.random.normal(jax.random.fold_in(key, 1), (ROWS, D), jnp.float32)
    subkeys = jax.random.split(jax.random.fold_in(key, 2), blocks)
    orders = jax.vmap(shuffle_rows)(subkeys)
    family = orders.reshape(PARTICLES)
    spread = 0.5 * jnp.exp(jax.random.uniform(jax.random.fold_in(key, 3), (PARTICLES, 1), jnp.float32, -0.6931472, 0.3364722))
    noise_key = jax.random.fold_in(key, 4)
    noise = jax.random.normal(noise_key, (PARTICLES, D), jnp.float32)
    points = 2.0 * protos[family] + 0.25 * centers[class_draw] + spread * noise
    return points.astype(jnp.bfloat16)


def draw_class_ids(key, part):
    class_draw, centers = crowd(key)
    return class_draw.astype(jnp.int32)


def draw_plan(key, part):
    key = jax.random.fold_in(key, 5)
    positions = jax.random.permutation(key, HOPS)[:ROUNDS].astype(jnp.int32)
    masks = jnp.left_shift(jnp.ones_like(positions), positions)
    blocks = jnp.arange(N_BLK, dtype=jnp.int32)
    return jnp.bitwise_xor(blocks[None, :], masks[:, None]).astype(jnp.int32)


def bell_draw(key, shape, scale, most, held_as=jnp.bfloat16):
    result = scale * jax.random.normal(key, shape, jnp.float32)
    return jnp.clip(result, min=-most, max=most).astype(held_as)


def setup_inputs(seed: int = 0, part: int = 0) -> dict:
    key_of = jax.random.split(jax.random.key(seed), 7)
    own_keys = jax.random.split(jax.random.fold_in(key_of[6], part), 7)
    return {
        "particles": draw_particles(jax.random.fold_in(jax.random.fold_in(key_of[6], part), 71), part),
        "class_ids": draw_class_ids(jax.random.fold_in(jax.random.fold_in(key_of[6], part), 71), part),
        "score_table": bell_draw(key_of[2], (CLASSES, D), 3.0, 18.0, jnp.float32),
        "precision": jnp.clip(jnp.exp(jax.random.uniform(key_of[3], (D,), jnp.float32, math.log(0.3), math.log(3.0))), 0.3, 3.0),
        "plan": draw_plan(jax.random.fold_in(key_of[6], 71), part),
        "median": jnp.clip(jax.random.uniform(own_keys[5], (1,), jnp.float32, 20.364676, 24.89016), 20.364676, 24.89016),
    }


def scores_of(ids, points, table, precision):
    return (table[ids] - precision[None, :] * points.astype(jnp.float32)).astype(jnp.bfloat16)


def tile_terms(left, right, right_scores, inv_t):
    gram = lax.dot_general(left, right, (((1,), (1,)), ((), ())), preferred_element_type=jnp.float32)
    left_wide = left.astype(jnp.float32)
    right_wide = right.astype(jnp.float32)
    squared = jnp.sum(left_wide * left_wide, axis=1)[:, None] + jnp.sum(right_wide * right_wide, axis=1)[None, :] - 2.0 * gram
    kernel = jnp.exp(-squared * inv_t).astype(jnp.bfloat16)
    kernel = lax.optimization_barrier(kernel)
    mass = jnp.sum(kernel.astype(jnp.float32), axis=1, keepdims=True)
    weighted = jnp.dot(kernel, right_scores, preferred_element_type=jnp.float32)
    moved = jnp.dot(kernel, right, preferred_element_type=jnp.float32)
    repulse = 2.0 * inv_t * (left_wide * mass - moved)
    return mass, weighted, repulse


def reference(particles, class_ids, score_table, precision, plan, median):
    inv_h = jnp.float32(math.log(1.0 + (ROUNDS + 1) * ROWS)) / (median[0] * median[0])
    scores = scores_of(class_ids, particles, score_table, precision)

    def one_block(block):
        start = (block * ROWS).astype(jnp.int32)
        left = lax.dynamic_slice_in_dim(particles, start, ROWS, 0)
        left_scores = lax.dynamic_slice_in_dim(scores, start, ROWS, 0)
        mass, weighted, repulse = tile_terms(left, left, left_scores, inv_h)
        for r in range(ROUNDS):
            other = (plan[r, block] * ROWS).astype(jnp.int32)
            right = lax.dynamic_slice_in_dim(particles, other, ROWS, 0)
            right_scores = lax.dynamic_slice_in_dim(scores, other, ROWS, 0)
            m, w, p = tile_terms(left, right, right_scores, inv_h / jnp.float32(r + 1))
            mass = mass + m
            weighted = weighted + w
            repulse = repulse + p
        return (weighted + repulse) / mass

    blocks = lax.map(one_block, jnp.arange(N_BLK, dtype=jnp.int32))
    return blocks.reshape(PARTICLES, D)
```

```python
import functools
import math

import jax
import jax.numpy as jnp
from jax import lax
from jax.experimental import pallas as pl
from jax.experimental.pallas import tpu as pltpu
from jax.sharding import PartitionSpec as P

ROUNDS = 4
CHUNKS = 2
LOG2E = math.log2(math.e)
F32, BF16 = jnp.float32, jnp.bfloat16


def flipped(index, bit):
    return index + (1 - 2 * ((index // (1 << bit)) % 2)) * (1 << bit)


def split_in_three(table):
    high = table.astype(BF16)
    rest = table - high.astype(F32)
    middle = rest.astype(BF16)
    low = (rest - middle.astype(F32)).astype(BF16)
    return jnp.concatenate([high, middle, low], axis=0)


def kernel(
    nbits,
    plan_ref,
    median_ref,
    x_hbm,
    ids_ref,
    table_ref,
    prec_ref,
    out_ref,
    own,
    slots,
    own_info,
    infos,
    norms,
    pieces,
    acc,
    mass,
    pulled,
    own_sem,
    send_sem,
    recv_sem,
    info_send,
    info_recv,
):
    rows, dims = own.shape
    size = rows // CHUNKS
    classes = table_ref.shape[0]
    me = lax.axis_index("blk")

    barrier = pltpu.get_barrier_semaphore()
    for bit in range(nbits):
        pl.semaphore_signal(
            barrier,
            inc=1,
            device_id={"blk": flipped(me, bit)},
            device_id_type=pl.DeviceIdType.MESH,
        )
    load = pltpu.make_async_copy(x_hbm, own, own_sem)
    load.start()
    pl.semaphore_wait(barrier, nbits)

    def block_copy(bit, chunk):
        part = pl.ds(chunk * size, size)
        return pltpu.make_async_remote_copy(
            src_ref=x_hbm.at[part],
            dst_ref=slots.at[bit, part],
            send_sem=send_sem.at[bit, chunk],
            recv_sem=recv_sem.at[bit, chunk],
            device_id={"blk": flipped(me, bit)},
            device_id_type=pl.DeviceIdType.MESH,
        )

    def info_copy(bit):
        return pltpu.make_async_remote_copy(
            src_ref=own_info,
            dst_ref=infos.at[bit],
            send_sem=info_send.at[bit],
            recv_sem=info_recv.at[bit],
            device_id={"blk": flipped(me, bit)},
            device_id_type=pl.DeviceIdType.MESH,
        )

    for chunk in range(CHUNKS):
        for bit in reversed(range(nbits)):
            block_copy(bit, chunk).start()

    load.wait()
    wide = own[...].astype(F32)
    half = 0.5 * jnp.sum(wide * wide, axis=1, keepdims=True)
    norms[...] = jnp.broadcast_to(half, norms.shape)
    half_row = jnp.transpose(norms[...])[0:8, :]
    ids_row = jnp.broadcast_to(ids_ref[...].astype(F32), half_row.shape)
    row = lax.broadcasted_iota(jnp.int32, half_row.shape, 0)
    own_info[...] = jnp.where(row == 0, ids_row, half_row)
    for bit in reversed(range(nbits)):
        info_copy(bit).start()

    pieces[...] = split_in_three(table_ref[...])
    acc[...] = jnp.zeros_like(acc)
    mass[...] = jnp.zeros_like(mass)
    pulled[...] = jnp.zeros_like(pulled)

    med = jnp.full((1, dims), median_ref[0], F32)
    inv_h = F32(math.log(1.0 + (ROUNDS + 1) * rows)) / (med * med)
    prec = prec_ref[...]

    def add_tile(right, info, share):
        inv = inv_h * share
        ids, half_right = info[0:1, :], info[1:2, :]
        number = lax.broadcasted_iota(jnp.int32, (classes, size), 0).astype(F32)
        onehot = jnp.transpose((number == ids).astype(F32)).astype(BF16)
        looked = jnp.dot(
            jnp.concatenate([onehot, onehot, onehot], axis=1),
            pieces[...],
            preferred_element_type=F32,
        )
        points = right.astype(F32)
        scores = (looked - prec * points).astype(BF16).astype(F32)
        pull = 2.0 * inv
        terms = (scores - pull * points).astype(BF16)
        gram = lax.dot_general(
            own[...], right, (((1,), (1,)), ((), ())), preferred_element_type=F32
        )
        left_half = jnp.concatenate([norms[...]] * (size // 128), axis=1)
        powers = ((gram - left_half) - half_right) * (pull[:, :size] * LOG2E)
        weights = jnp.exp2(powers).astype(BF16)
        acc[...] += jnp.dot(weights, terms, preferred_element_type=F32)
        wide_weights = weights.astype(F32)
        part = wide_weights[:, :128]
        for lane in range(128, size, 128):
            part = part + wide_weights[:, lane : lane + 128]
        mass[...] += part
        pulled[...] += part * pull[:, :128]

    for chunk in range(CHUNKS):
        part = pl.ds(chunk * size, size)
        add_tile(own[part, :], own_info[:, part], F32(1.0))

    def share_of_bit(bit):
        share = F32(0.0)
        for step in range(ROUNDS):
            share = jnp.where(plan_ref[step, 0] == (1 << bit), F32(1.0 / (step + 1)), share)
        return share

    if nbits == ROUNDS:
        near = min(2, nbits)
        order = [(bit, chunk) for bit in range(near) for chunk in range(CHUNKS)]
        order += [(bit, chunk) for chunk in range(CHUNKS) for bit in range(near, nbits)]
        for bit in range(near):
            info_copy(bit).wait_recv()
        for place, (bit, chunk) in enumerate(order):
            if place == near * CHUNKS:
                for later in range(near, nbits):
                    info_copy(later).wait_recv()
            block_copy(bit, chunk).wait_recv()
            part = pl.ds(chunk * size, size)
            add_tile(slots[bit, part, :], infos[bit, :, part], share_of_bit(bit))
    else:
        for bit in range(nbits):
            info_copy(bit).wait_recv()
            for chunk in range(CHUNKS):
                block_copy(bit, chunk).wait_recv()
        for step in range(ROUNDS):
            slot = jnp.int32(0)
            for bit in range(nbits):
                slot = jnp.where(plan_ref[step, 0] == (1 << bit), jnp.int32(bit), slot)
            for chunk in range(CHUNKS):
                part = pl.ds(chunk * size, size)
                add_tile(slots[slot, part, :], infos[slot, :, part], F32(1.0 / (step + 1)))

    total = jnp.sum(mass[...], axis=1, keepdims=True)
    pull_total = jnp.sum(pulled[...], axis=1, keepdims=True)
    out_ref[...] = (acc[...] + own[...].astype(F32) * pull_total) / total

    for bit in range(nbits):
        info_copy(bit).wait_send()
        for chunk in range(CHUNKS):
            block_copy(bit, chunk).wait_send()


def per_device(particles, class_ids, score_table, precision, plan, median):
    rows, dims = particles.shape
    nbits = lax.axis_size("blk").bit_length() - 1
    vmem = pl.BlockSpec(memory_space=pltpu.VMEM)
    smem = pl.BlockSpec(memory_space=pltpu.SMEM)
    return pl.pallas_call(
        functools.partial(kernel, nbits),
        out_shape=jax.ShapeDtypeStruct((rows, dims), F32),
        in_specs=[smem, smem, pl.BlockSpec(memory_space=pl.ANY), vmem, vmem, vmem],
        out_specs=vmem,
        scratch_shapes=[
            pltpu.VMEM((rows, dims), BF16),
            pltpu.VMEM((nbits, rows, dims), BF16),
            pltpu.VMEM((8, rows), F32),
            pltpu.VMEM((nbits, 8, rows), F32),
            pltpu.VMEM((rows, 128), F32),
            pltpu.VMEM((3 * score_table.shape[0], dims), BF16),
            pltpu.VMEM((rows, dims), F32),
            pltpu.VMEM((rows, 128), F32),
            pltpu.VMEM((rows, 128), F32),
            pltpu.SemaphoreType.DMA,
            pltpu.SemaphoreType.DMA((nbits, CHUNKS)),
            pltpu.SemaphoreType.DMA((nbits, CHUNKS)),
            pltpu.SemaphoreType.DMA((nbits,)),
            pltpu.SemaphoreType.DMA((nbits,)),
        ],
        compiler_params=pltpu.CompilerParams(
            collective_id=0, has_side_effects=True, vmem_limit_bytes=32 * 1024 * 1024
        ),
        name="stein_drift",
    )(
        plan,
        median,
        particles,
        class_ids.reshape(1, rows),
        score_table,
        precision.reshape(1, dims),
    )


def solution(mesh):
    placed = (P(("groups", "blk"), None), P(("groups", "blk")), P(), P(), P(), P("groups"))
    return jax.shard_map(
        per_device,
        mesh=mesh,
        in_specs=placed,
        out_specs=P(("groups", "blk"), None),
        check_vma=False,
    )
```

```python
import functools
import math

import jax
import jax.numpy as jnp
from jax import lax
from jax.experimental import pallas as pl
from jax.experimental.pallas import tpu as pltpu
from jax.sharding import PartitionSpec as P

ROUNDS = 4
CHUNKS = 4
LOG2E = math.log2(math.e)
F32, BF16 = jnp.float32, jnp.bfloat16


def flipped(index, bit):
    return index + (1 - 2 * ((index // (1 << bit)) % 2)) * (1 << bit)


def split_in_three(table):
    high = table.astype(BF16)
    rest = table - high.astype(F32)
    middle = rest.astype(BF16)
    low = (rest - middle.astype(F32)).astype(BF16)
    return jnp.concatenate([high, middle, low], axis=0)


def kernel(
    nbits,
    x_hbm,
    ids_hbm,
    table_hbm,
    prec_hbm,
    median_hbm,
    plan_hbm,
    out_ref,
    own,
    ids_ref,
    table_ref,
    prec_ref,
    median_ref,
    plan_ref,
    slots,
    own_info,
    infos,
    looked,
    norms,
    pieces,
    acc,
    mass,
    pulled,
    own_sem,
    send_sem,
    recv_sem,
    info_send,
    info_recv,
):
    rows, dims = own.shape
    size = rows // CHUNKS
    classes = table_ref.shape[0]
    me = lax.axis_index("blk")

    barrier = pltpu.get_barrier_semaphore()
    for bit in range(nbits):
        pl.semaphore_signal(
            barrier,
            inc=1,
            device_id={"blk": flipped(me, bit)},
            device_id_type=pl.DeviceIdType.MESH,
        )
    sources = (x_hbm, ids_hbm, table_hbm, prec_hbm, median_hbm, plan_hbm)
    copies = (own, ids_ref, table_ref, prec_ref, median_ref, plan_ref)
    loads = [
        pltpu.make_async_copy(source, copy, own_sem.at[place])
        for place, (source, copy) in enumerate(zip(sources, copies))
    ]
    for load in loads:
        load.start()
    for load in loads:
        load.wait()

    wide = own[...].astype(F32)
    half = 0.5 * jnp.sum(wide * wide, axis=1, keepdims=True)
    norms[...] = jnp.broadcast_to(half, norms.shape)
    half_row = jnp.transpose(norms[...])[0:2, :]
    ids_row = jnp.broadcast_to(ids_ref[...].astype(F32), half_row.shape)
    row = lax.broadcasted_iota(jnp.int32, half_row.shape, 0)
    own_info[...] = jnp.where(row == 0, ids_row, half_row)

    pl.semaphore_wait(barrier, nbits)

    def block_copy(bit, chunk):
        part = pl.ds(chunk * size, size)
        return pltpu.make_async_remote_copy(
            src_ref=x_hbm.at[part],
            dst_ref=slots.at[bit, part],
            send_sem=send_sem.at[bit, chunk],
            recv_sem=recv_sem.at[bit, chunk],
            device_id={"blk": flipped(me, bit)},
            device_id_type=pl.DeviceIdType.MESH,
        )

    def info_copy(bit):
        return pltpu.make_async_remote_copy(
            src_ref=own_info,
            dst_ref=infos.at[bit],
            send_sem=info_send.at[bit],
            recv_sem=info_recv.at[bit],
            device_id={"blk": flipped(me, bit)},
            device_id_type=pl.DeviceIdType.MESH,
        )

    for bit in reversed(range(nbits)):
        info_copy(bit).start()
    for chunk in range(CHUNKS):
        for bit in reversed(range(nbits)):
            block_copy(bit, chunk).start()
    pieces[...] = split_in_three(table_ref[...])
    acc[...] = jnp.zeros_like(acc)
    mass[...] = jnp.zeros_like(mass)
    pulled[...] = jnp.zeros_like(pulled)
    med = jnp.full((1, 1), median_ref[0], F32)
    inv_h = F32(math.log(1.0 + (ROUNDS + 1) * rows)) / (med * med)
    prec = prec_ref[...]

    def look_up(ids):
        number = lax.broadcasted_iota(jnp.int32, (classes, ids.shape[1]), 0).astype(F32)
        onehot = jnp.transpose((number == ids).astype(F32)).astype(BF16)
        return jnp.dot(
            jnp.concatenate([onehot, onehot, onehot], axis=1),
            pieces[...],
            preferred_element_type=F32,
        )

    def add_tile(right, offsets, half_right, share):
        count = right.shape[0]
        pull = (2.0 * inv_h) * share
        points = right.astype(F32)
        scores = (offsets - prec * points).astype(BF16).astype(F32)
        terms = (scores - jnp.broadcast_to(pull, (1, dims)) * points).astype(BF16)
        gram = lax.dot_general(
            own[...], right, (((1,), (1,)), ((), ())), preferred_element_type=F32
        )
        left_half = jnp.concatenate([norms[...]] * (count // 128), axis=1)
        scale = jnp.broadcast_to(pull * LOG2E, (1, count))
        weights = jnp.exp2(((gram - left_half) - half_right) * scale).astype(BF16)
        acc[...] += jnp.dot(weights, terms, preferred_element_type=F32)
        wide_weights = weights.astype(F32)
        part = wide_weights[:, :128]
        for lane in range(128, count, 128):
            part = part + wide_weights[:, lane : lane + 128]
        mass[...] += part
        pulled[...] += part * jnp.broadcast_to(pull, (1, 128))

    wide_size = rows // 2
    for half_block in range(2):
        part = pl.ds(half_block * wide_size, wide_size)
        add_tile(own[part, :], look_up(own_info[0:1, part]), own_info[1:2, part], F32(1.0))

    for bit in range(nbits):
        info_copy(bit).wait_recv()
        looked[bit] = look_up(infos[bit, 0:1, :])

    def add_part(slot, start, count, share):
        part = pl.ds(start, count)
        add_tile(slots[slot, part, :], looked[slot, part, :], infos[slot, 1:2, part], share)

    def share_of_bit(bit):
        share = F32(0.0)
        for step in range(ROUNDS):
            share = jnp.where(plan_ref[step, 0] == (1 << bit), F32(1.0 / (step + 1)), share)
        return share

    if nbits == ROUNDS:
        near = nbits // 2
        for bit in range(near):
            for half_block in range(2):
                for chunk in range(half_block * CHUNKS // 2, (half_block + 1) * CHUNKS // 2):
                    block_copy(bit, chunk).wait_recv()
                add_part(bit, half_block * wide_size, wide_size, share_of_bit(bit))
        for chunk in range(CHUNKS):
            for bit in reversed(range(near, nbits)):
                block_copy(bit, chunk).wait_recv()
                add_part(bit, chunk * size, size, share_of_bit(bit))
    else:
        for bit in range(nbits):
            for chunk in range(CHUNKS):
                block_copy(bit, chunk).wait_recv()
        for step in range(ROUNDS):
            slot = jnp.int32(0)
            for bit in range(nbits):
                slot = jnp.where(plan_ref[step, 0] == (1 << bit), jnp.int32(bit), slot)
            for half_block in range(2):
                add_part(slot, half_block * wide_size, wide_size, F32(1.0 / (step + 1)))

    scale = 1.0 / jnp.sum(mass[...], axis=1, keepdims=True)
    pull_total = jnp.sum(pulled[...], axis=1, keepdims=True)
    out_ref[...] = (acc[...] + own[...].astype(F32) * pull_total) * scale

    for bit in range(nbits):
        info_copy(bit).wait_send()
        for chunk in range(CHUNKS):
            block_copy(bit, chunk).wait_send()


def per_device(particles, class_ids, score_table, precision, plan, median):
    rows, dims = particles.shape
    nbits = lax.axis_size("blk").bit_length() - 1
    vmem = pl.BlockSpec(memory_space=pltpu.VMEM)
    hbm = pl.BlockSpec(memory_space=pltpu.HBM)
    return pl.pallas_call(
        functools.partial(kernel, nbits),
        out_shape=pltpu.VMEM((rows, dims), F32),
        in_specs=[hbm] * 6,
        out_specs=vmem,
        scratch_shapes=[
            pltpu.VMEM((rows, dims), BF16),
            pltpu.VMEM((1, rows), jnp.int32),
            pltpu.VMEM(score_table.shape, F32),
            pltpu.VMEM((1, dims), F32),
            pltpu.SMEM((1,), F32),
            pltpu.SMEM(plan.shape, jnp.int32),
            pltpu.VMEM((nbits, rows, dims), BF16),
            pltpu.VMEM((2, rows), F32),
            pltpu.VMEM((nbits, 2, rows), F32),
            pltpu.VMEM((nbits, rows, dims), F32),
            pltpu.VMEM((rows, 128), F32),
            pltpu.VMEM((3 * score_table.shape[0], dims), BF16),
            pltpu.VMEM((rows, dims), F32),
            pltpu.VMEM((rows, 128), F32),
            pltpu.VMEM((rows, 128), F32),
            pltpu.SemaphoreType.DMA((6,)),
            pltpu.SemaphoreType.DMA((nbits, CHUNKS)),
            pltpu.SemaphoreType.DMA((nbits, CHUNKS)),
            pltpu.SemaphoreType.DMA((nbits,)),
            pltpu.SemaphoreType.DMA((nbits,)),
        ],
        compiler_params=pltpu.CompilerParams(
            collective_id=0, has_side_effects=True, vmem_limit_bytes=60 * 1024 * 1024
        ),
        name="stein_drift",
    )(
        particles,
        class_ids.reshape(1, rows),
        score_table,
        precision.reshape(1, dims),
        median,
        plan,
    )


def solution(mesh):
    placed = (P(("groups", "blk"), None), P(("groups", "blk")), P(), P(), P(), P("groups"))
    return jax.shard_map(
        per_device,
        mesh=mesh,
        in_specs=placed,
        out_specs=P(("groups", "blk"), None),
        check_vma=False,
    )
```

```python
import functools
import math

import jax
import jax.numpy as jnp
from jax import lax
from jax.experimental import pallas as pl
from jax.experimental.pallas import tpu as pltpu
from jax.sharding import PartitionSpec as P

ROUNDS = 4
CHUNKS = 4
LOG2E = math.log2(math.e)
F32, BF16 = jnp.float32, jnp.bfloat16


def flipped(index, bit):
    return index + (1 - 2 * ((index // (1 << bit)) % 2)) * (1 << bit)


def split_in_three(table):
    high = table.astype(BF16)
    rest = table - high.astype(F32)
    middle = rest.astype(BF16)
    low = (rest - middle.astype(F32)).astype(BF16)
    return jnp.concatenate([high, middle, low], axis=0)


def kernel(
    nbits,
    x_hbm,
    ids_hbm,
    table_hbm,
    prec_hbm,
    median_hbm,
    plan_hbm,
    out_ref,
    own,
    ids_ref,
    table_ref,
    prec_ref,
    median_ref,
    plan_ref,
    slots,
    own_info,
    infos,
    looked,
    norms,
    pieces,
    acc,
    mass,
    pulled,
    own_sem,
    send_sem,
    recv_sem,
    info_send,
    info_recv,
):
    rows, dims = own.shape
    size = rows // CHUNKS
    classes = table_ref.shape[0]
    me = lax.axis_index("blk")

    barrier = pltpu.get_barrier_semaphore()
    for bit in range(nbits):
        pl.semaphore_signal(
            barrier,
            inc=1,
            device_id={"blk": flipped(me, bit)},
            device_id_type=pl.DeviceIdType.MESH,
        )
    sources = (x_hbm, ids_hbm, table_hbm, prec_hbm, median_hbm, plan_hbm)
    copies = (own, ids_ref, table_ref, prec_ref, median_ref, plan_ref)
    loads = [
        pltpu.make_async_copy(source, copy, own_sem.at[place])
        for place, (source, copy) in enumerate(zip(sources, copies))
    ]
    for load in loads:
        load.start()
    for load in loads:
        load.wait()

    wide = own[...].astype(F32)
    half = 0.5 * jnp.sum(wide * wide, axis=1, keepdims=True)
    norms[...] = jnp.broadcast_to(half, norms.shape)
    half_row = jnp.transpose(norms[...])[0:2, :]
    ids_row = jnp.broadcast_to(ids_ref[...].astype(F32), half_row.shape)
    row = lax.broadcasted_iota(jnp.int32, half_row.shape, 0)
    own_info[...] = jnp.where(row == 0, ids_row, half_row)

    pl.semaphore_wait(barrier, nbits)

    def block_copy(bit, chunk):
        part = pl.ds(chunk * size, size)
        return pltpu.make_async_remote_copy(
            src_ref=x_hbm.at[part],
            dst_ref=slots.at[bit, part],
            send_sem=send_sem.at[bit, chunk],
            recv_sem=recv_sem.at[bit, chunk],
            device_id={"blk": flipped(me, bit)},
            device_id_type=pl.DeviceIdType.MESH,
        )

    def info_copy(bit):
        return pltpu.make_async_remote_copy(
            src_ref=own_info,
            dst_ref=infos.at[bit],
            send_sem=info_send.at[bit],
            recv_sem=info_recv.at[bit],
            device_id={"blk": flipped(me, bit)},
            device_id_type=pl.DeviceIdType.MESH,
        )

    for bit in reversed(range(nbits)):
        info_copy(bit).start()
    for chunk in range(CHUNKS):
        block_copy(nbits - 1, chunk).start()
    for chunk in range(CHUNKS):
        for bit in reversed(range(nbits - 1)):
            block_copy(bit, chunk).start()
    pieces[...] = split_in_three(table_ref[...])
    acc[...] = jnp.zeros_like(acc)
    mass[...] = jnp.zeros_like(mass)
    pulled[...] = jnp.zeros_like(pulled)
    med = jnp.full((1, 1), median_ref[0], F32)
    inv_h = F32(math.log(1.0 + (ROUNDS + 1) * rows)) / (med * med)
    prec = prec_ref[...]

    def look_up(ids):
        number = lax.broadcasted_iota(jnp.int32, (classes, ids.shape[1]), 0).astype(F32)
        onehot = jnp.transpose((number == ids).astype(F32)).astype(BF16)
        return jnp.dot(
            jnp.concatenate([onehot, onehot, onehot], axis=1),
            pieces[...],
            preferred_element_type=F32,
        )

    def add_tile(right, offsets, half_right, share):
        count = right.shape[0]
        pull = (2.0 * inv_h) * share
        points = right.astype(F32)
        scores = (offsets - prec * points).astype(BF16).astype(F32)
        terms = (scores - jnp.broadcast_to(pull, (1, dims)) * points).astype(BF16)
        gram = lax.dot_general(
            own[...], right, (((1,), (1,)), ((), ())), preferred_element_type=F32
        )
        left_half = jnp.concatenate([norms[...]] * (count // 128), axis=1)
        scale = jnp.broadcast_to(pull * LOG2E, (1, count))
        weights = jnp.exp2(((gram - left_half) - half_right) * scale).astype(BF16)
        acc[...] += jnp.dot(weights, terms, preferred_element_type=F32)
        wide_weights = weights.astype(F32)
        part = wide_weights[:, :128]
        for lane in range(128, count, 128):
            part = part + wide_weights[:, lane : lane + 128]
        mass[...] += part
        pulled[...] += part * jnp.broadcast_to(pull, (1, 128))

    wide_size = rows // 2
    for half_block in range(2):
        part = pl.ds(half_block * wide_size, wide_size)
        add_tile(own[part, :], look_up(own_info[0:1, part]), own_info[1:2, part], F32(1.0))

    for bit in range(nbits):
        info_copy(bit).wait_recv()
        looked[bit] = look_up(infos[bit, 0:1, :])

    def add_part(slot, start, count, share):
        part = pl.ds(start, count)
        add_tile(slots[slot, part, :], looked[slot, part, :], infos[slot, 1:2, part], share)

    def share_of_bit(bit):
        share = F32(0.0)
        for step in range(ROUNDS):
            share = jnp.where(plan_ref[step, 0] == (1 << bit), F32(1.0 / (step + 1)), share)
        return share

    if nbits == ROUNDS:
        near = nbits - 1
        for bit in range(near):
            for half_block in range(2):
                for chunk in range(half_block * CHUNKS // 2, (half_block + 1) * CHUNKS // 2):
                    block_copy(bit, chunk).wait_recv()
                add_part(bit, half_block * wide_size, wide_size, share_of_bit(bit))
        for chunk in range(CHUNKS):
            for bit in reversed(range(near, nbits)):
                block_copy(bit, chunk).wait_recv()
                add_part(bit, chunk * size, size, share_of_bit(bit))
    else:
        for bit in range(nbits):
            for chunk in range(CHUNKS):
                block_copy(bit, chunk).wait_recv()
        for step in range(ROUNDS):
            slot = jnp.int32(0)
            for bit in range(nbits):
                slot = jnp.where(plan_ref[step, 0] == (1 << bit), jnp.int32(bit), slot)
            for half_block in range(2):
                add_part(slot, half_block * wide_size, wide_size, F32(1.0 / (step + 1)))

    scale = 1.0 / jnp.sum(mass[...], axis=1, keepdims=True)
    pull_total = jnp.sum(pulled[...], axis=1, keepdims=True)
    out_ref[...] = (acc[...] + own[...].astype(F32) * pull_total) * scale

    for bit in range(nbits):
        info_copy(bit).wait_send()
        for chunk in range(CHUNKS):
            block_copy(bit, chunk).wait_send()


def per_device(particles, class_ids, score_table, precision, plan, median):
    rows, dims = particles.shape
    nbits = lax.axis_size("blk").bit_length() - 1
    vmem = pl.BlockSpec(memory_space=pltpu.VMEM)
    hbm = pl.BlockSpec(memory_space=pltpu.HBM)
    return pl.pallas_call(
        functools.partial(kernel, nbits),
        out_shape=pltpu.VMEM((rows, dims), F32),
        in_specs=[hbm] * 6,
        out_specs=vmem,
        scratch_shapes=[
            pltpu.VMEM((rows, dims), BF16),
            pltpu.VMEM((1, rows), jnp.int32),
            pltpu.VMEM(score_table.shape, F32),
            pltpu.VMEM((1, dims), F32),
            pltpu.SMEM((1,), F32),
            pltpu.SMEM(plan.shape, jnp.int32),
            pltpu.VMEM((nbits, rows, dims), BF16),
            pltpu.VMEM((2, rows), F32),
            pltpu.VMEM((nbits, 2, rows), F32),
            pltpu.VMEM((nbits, rows, dims), F32),
            pltpu.VMEM((rows, 128), F32),
            pltpu.VMEM((3 * score_table.shape[0], dims), BF16),
            pltpu.VMEM((rows, dims), F32),
            pltpu.VMEM((rows, 128), F32),
            pltpu.VMEM((rows, 128), F32),
            pltpu.SemaphoreType.DMA((6,)),
            pltpu.SemaphoreType.DMA((nbits, CHUNKS)),
            pltpu.SemaphoreType.DMA((nbits, CHUNKS)),
            pltpu.SemaphoreType.DMA((nbits,)),
            pltpu.SemaphoreType.DMA((nbits,)),
        ],
        compiler_params=pltpu.CompilerParams(
            collective_id=0, has_side_effects=True, vmem_limit_bytes=60 * 1024 * 1024
        ),
        name="stein_drift",
    )(
        particles,
        class_ids.reshape(1, rows),
        score_table,
        precision.reshape(1, dims),
        median,
        plan,
    )


def solution(mesh):
    placed = (P(("groups", "blk"), None), P(("groups", "blk")), P(), P(), P(), P("groups"))
    return jax.shard_map(
        per_device,
        mesh=mesh,
        in_specs=placed,
        out_specs=P(("groups", "blk"), None),
        check_vma=False,
    )
```
